256 devices in a mesh: rows: 64 (over y, z, core), rhs: 4 (over x).
Axes of the slice: x: 4, y: 4, z: 8, core: 2. Of those that a mesh axis runs over, the one named last changes fastest.
Arguments:
- right_side: bfloat16 [512, 512, 256], P('rows', 'rhs'), may hold values from -6 to 6
- off_blocks: bfloat16 [512, 8, 256, 256], P('rows', None, 'rhs'), may hold values from -0.125 to 0.125
- diag_inverse: bfloat16 [512, 256, 256], P('rows', 'rhs'), may hold values from -0.375 to 0.375
- block_level: int32 [512], P('rows'), may hold values from 0 to 3, as said below
- block_columns: int32 [512, 8], P('rows'), may hold values from 0 to 511, as said below
Outputs:
- solved: bfloat16 [512, 512, 256], P('rows', 'rhs')
The draws below stay inside these ranges and needn't reach their ends.
Inputs may be any that keep to these rules, and one draw needn't show every extreme that they name: `block_level`: among the 8 block rows of one index of rows every level occurs, none more than 4 times, and one level exactly 4 times. `block_columns`: block row i lies on index i // 8 of rows; each of its 8 block columns is a block row on the same index or one of the 3 indices below it (none below 0), of lower level when block row i has level 1 or more. Columns of one block row may repeat.
All inputs are finite; a program needn't handle non-finite values.
Results may differ from the reference program's by a relative error of at most 0.0075.
Values may be sent and summed in bfloat16 or wider, within the bound.
No kernel may reach another device: no remote copies, remote signals or barrier semaphores. Data moves between devices by JAX's collectives and lax.ppermute only.
A program may use at most 128 MiB of HBM per device.

```python
import jax
import jax.numpy as jnp
from jax import lax

BS = 256
K = 8
LEVELS = 4
REACH = 4
BR_DEV = 8
CAP = 4
NB = 512
RHS = 512


def level_table(key):
    groups = NB // BR_DEV
    heavy_key = jax.random.fold_in(key, 101)
    rest_key = jax.random.fold_in(key, 102)
    order_key = jax.random.fold_in(key, 103)
    heavy = jax.random.randint(heavy_key, (groups,), 0, LEVELS)
    each_once = (heavy[:, None] + 1 + jnp.arange(LEVELS - 1, dtype=jnp.int32)[None, :]) % LEVELS
    extra = BR_DEV - CAP - (LEVELS - 1)
    others = jax.random.randint(rest_key, (groups, extra), 0, LEVELS - 1)
    others = (heavy[:, None] + 1 + others) % LEVELS
    slots = jnp.concatenate([jnp.broadcast_to(heavy[:, None], (groups, CAP)), each_once, others], axis=1)
    scores = jax.random.randint(order_key, (groups, BR_DEV), 0, 2 ** 20) * BR_DEV
    scores = scores + jnp.arange(BR_DEV, dtype=jnp.int32)[None, :]
    ranking = jnp.argsort(scores, axis=1)
    return jnp.take_along_axis(slots, ranking, axis=1).reshape(NB).astype(jnp.int32)


def draw_block_level(key, part):
    return level_table(key)


def draw_block_columns(key, part):
    levels = level_table(key)
    key = jax.random.fold_in(key, 7)
    column_ids = jnp.arange(NB, dtype=jnp.int32)
    owner = column_ids // BR_DEV
    near = (owner[None, :] <= owner[:, None]) & (owner[None, :] > owner[:, None] - REACH)
    lower = (levels[None, :] < levels[:, None]) | (levels[:, None] == 0)
    allowed = near & lower
    scores = jax.random.randint(key, (NB, K, NB), 0, 2 ** 16) * NB + column_ids[None, None, :]
    scores = jnp.where(allowed[:, None, :], scores, -1)
    chosen = jnp.argmax(scores, axis=2)
    return chosen.astype(jnp.int32)


def shard_levels(rng, extent, split, low, largest):
    level, own = 1.0, jax.random.fold_in(rng, 6)
    for axis_at, parts in split:
        heights = jnp.exp(jax.random.uniform(jax.random.fold_in(own, axis_at), (parts,), jnp.float32, low / len(split), largest / len(split)))
        level = level * jnp.repeat(heights, extent[axis_at] // parts).reshape([-1 if axis == axis_at else 1 for axis in range(len(extent))])
    return level


def centred(own_key, shape, deviation, most, pieces=(), held_as=jnp.bfloat16):
    array = jax.random.normal(own_key, shape, jnp.float32) * deviation
    if len(pieces) > 0:
        array = shard_levels(own_key, shape, pieces, -0.22, 0.18) * array
    return jnp.clip(array, min=-most, max=most).astype(held_as)


def setup_inputs(seed: int = 0) -> dict:
    seeds = jax.random.split(jax.random.key(seed), 6)
    right_side = centred(seeds[0], (NB, RHS, BS), 1.0, 6.0, ((0, 64), (1, 4)))
    off_blocks = centred(seeds[1], (NB, K, BS, BS), (BS * K) ** -0.5, 0.125, ((0, 64), (2, 4)))
    diag_inverse = centred(seeds[2], (NB, BS, BS), BS ** -0.5, 0.375, ((0, 64), (1, 4)))
    block_level = draw_block_level(jax.random.fold_in(seeds[5], 71), 0)
    block_columns = draw_block_columns(jax.random.fold_in(seeds[5], 71), 0)
    return {"right_side": right_side, "off_blocks": off_blocks, "diag_inverse": diag_inverse, "block_level": block_level, "block_columns": block_columns}


def reference(right_side, off_blocks, diag_inverse, block_level, block_columns):
    solved = jnp.zeros(right_side.shape, jnp.bfloat16)
    for level_now in range(LEVELS):
        def one_row(items, current=solved):
            blocks, inverse, rhs_row, cols_row = items
            picked = jnp.take(current, cols_row.astype(jnp.int32), axis=0).astype(jnp.float32)
            contribution = jnp.einsum("krb,kab->ra", picked, blocks.astype(jnp.float32))
            residue = (rhs_row.astype(jnp.float32) - contribution).astype(jnp.bfloat16)
            residue = lax.optimization_barrier(residue)
            updated = jnp.einsum("rb,ab->ra", residue.astype(jnp.float32), inverse.astype(jnp.float32))
            return updated.astype(jnp.bfloat16)

        updated = lax.map(one_row, (off_blocks, diag_inverse, right_side, block_columns))
        solved = jnp.where((block_level == level_now)[:, None, None], updated, solved)
        solved = lax.optimization_barrier(solved)
    return solved
```

```python
import functools

import jax
import jax.numpy as jnp
from jax import lax
from jax.experimental import pallas as pl
from jax.experimental.pallas import tpu as pltpu
from jax.sharding import PartitionSpec as P

LEVELS = 4
REACH = 4
CAP = 4
ANY = pl.BlockSpec(memory_space=pl.ANY)
SMEM = pl.BlockSpec(memory_space=pltpu.SMEM)
VMEM = pl.BlockSpec(memory_space=pltpu.VMEM)
PARAMS = pltpu.CompilerParams(vmem_limit_bytes=24 * 2**20)

PLACES = {1: range(0, 4), 2: range(1, 6), 3: range(2, 7), 0: range(4, 8)}
CHUNKS = ((0, 2), (2, 4), (4, 6), (6, 7))
FORWARD = (True, True, False, False)


def order_of(level_ref, order_ref):
    at = jnp.int32(0)
    starts = {}
    for level in (1, 2, 3, 0):
        starts[level] = at
        for row in range(8):
            here = level_ref[row] == level

            @pl.when(here)
            def _(at=at, row=row):
                order_ref[at] = jnp.int32(row)

            at = at + here.astype(jnp.int32)
    return starts


def sort_kernel(level_ref, off_ref, *refs):
    chunks, (order_ref, sems) = refs[: len(CHUNKS)], refs[len(CHUNKS) :]
    order_of(level_ref, order_ref)
    copies = []
    for chunk_ref, (low, high) in zip(chunks, CHUNKS):
        for place in range(low, high):
            copies.append(
                pltpu.make_async_copy(off_ref.at[order_ref[place]], chunk_ref.at[place - low], sems.at[place])
            )
    for copy in copies:
        copy.start()
    for copy in copies:
        copy.wait()


def sort_call(level, off):
    return pl.pallas_call(
        sort_kernel,
        out_shape=[jax.ShapeDtypeStruct((high - low,) + off.shape[1:], off.dtype) for low, high in CHUNKS],
        in_specs=[SMEM, ANY],
        out_specs=[VMEM] * len(CHUNKS),
        scratch_shapes=[pltpu.SMEM((8,), jnp.int32), pltpu.SemaphoreType.DMA((8,))],
        compiler_params=PARAMS,
    )(level, off)


TABLE = 80
TAIL = 16


def table_kernel(rows_at_ref, level_ref, columns_ref, one_ref, two_ref, three_ref, table_ref, slot_ref, levels_ref, near_ref, sem):
    parts = [
        ref[ref.shape[0] - TAIL :, :128].astype(jnp.float32).astype(jnp.int32)[:8] for ref in (one_ref, two_ref, three_ref)
    ]
    lane = lax.broadcasted_iota(jnp.int32, (8, 128), 0)
    levels_ref[...] = jnp.where(lane == 0, parts[0], jnp.where(lane == 1, parts[1], parts[2]))
    copy = pltpu.make_async_copy(levels_ref, near_ref, sem)
    copy.start()
    starts = order_of(level_ref, table_ref)
    ends = {1: starts[2], 2: starts[3], 3: starts[0], 0: jnp.int32(8)}
    for level in range(LEVELS):
        table_ref[8 + level] = starts[level]
        table_ref[12 + level] = ends[level]
    copy.wait()
    for distance in range(REACH):
        seen = [jnp.int32(0)] * LEVELS
        for row in range(8):
            level = level_ref[row] if distance == 0 else near_ref[distance - 1, row] & 3
            rank = jnp.int32(0)
            for other in range(LEVELS):
                here = level == other
                rank = jnp.where(here, seen[other], rank)
                seen[other] = seen[other] + here.astype(jnp.int32)
            slot_ref[distance * 8 + row] = 16 * jnp.minimum(level, 2) + 4 * distance + jnp.minimum(rank, CAP - 1)
    base = rows_at_ref[0]
    for place in range(7):
        row = table_ref[place]
        for k in range(8):
            column = columns_ref[row, k]
            distance = jnp.clip(base - lax.shift_right_logical(column, 3), 0, REACH - 1)
            table_ref[16 + 8 * place + k] = slot_ref[distance * 8 + (column & 7)]


def table_call(rows_at, level, columns, received):
    return pl.pallas_call(
        table_kernel,
        out_shape=jax.ShapeDtypeStruct((TABLE,), jnp.int32),
        in_specs=[SMEM] * 3 + [VMEM] * 3,
        out_specs=SMEM,
        scratch_shapes=[
            pltpu.SMEM((32,), jnp.int32),
            pltpu.VMEM((8, 128), jnp.int32),
            pltpu.SMEM((8, 128), jnp.int32),
            pltpu.SemaphoreType.DMA,
        ],
        compiler_params=PARAMS,
    )(rows_at, level, columns, *received)


def dot_t(x, y):
    return lax.dot_general(x, y, (((1,), (1,)), ((), ())), preferred_element_type=jnp.float32)


def in_order(x_at, total):
    return pltpu.roll(total, lax.rem(x_at + 3, 4) * 64, 1)


def first_kernel(x_ref, level_ref, right_ref, own_ref, before_ref, after_ref, across_ref, out_ref, solved_ref, order_ref, sems):
    x_at = x_ref[0]
    columns = right_ref.shape[1]
    begin = order_of(level_ref, order_ref)[0]

    def store(place):
        at = pl.multiple_of((place - begin) * columns, columns)
        return pltpu.make_async_copy(
            solved_ref.at[pl.ds(at, columns)], out_ref.at[order_ref[place]], sems.at[place - 4]
        )

    lane = lax.broadcasted_iota(jnp.int32, (TAIL, 256), 1)
    tail = jnp.zeros((TAIL, 256), jnp.int32)
    for row in range(8):
        tail = jnp.where(lane == row, level_ref[row], tail)
    solved_ref[CAP * columns :] = tail.astype(jnp.float32).astype(solved_ref.dtype)
    for place in PLACES[0]:

        @pl.when(place >= begin)
        def _(place=place):
            row = order_ref[place]
            inverse = jnp.concatenate([ref[row] for ref in (before_ref, own_ref, after_ref, across_ref)], axis=0)
            updated = in_order(x_at, dot_t(right_ref[row], inverse)).astype(solved_ref.dtype)
            solved_ref[pl.ds(pl.multiple_of((place - begin) * columns, columns), columns)] = updated
            store(place).start()

    for place in PLACES[0]:

        @pl.when(place >= begin)
        def _(place=place):
            store(place).wait()


def first_call(x_at, level, right, diag_pieces):
    rows, columns, size = right.shape
    return pl.pallas_call(
        first_kernel,
        out_shape=[
            jax.ShapeDtypeStruct(right.shape, right.dtype),
            jax.ShapeDtypeStruct((CAP * columns + TAIL, size), right.dtype),
        ],
        in_specs=[SMEM, SMEM] + [VMEM] * 5,
        out_specs=[ANY, VMEM],
        scratch_shapes=[pltpu.SMEM((8,), jnp.int32), pltpu.SemaphoreType.DMA((CAP,))],
        compiler_params=PARAMS,
        cost_estimate=pl.CostEstimate(flops=2 * CAP * columns * size * size, bytes_accessed=3 * 2**20, transcendentals=0),
    )(x_at, level, right, *diag_pieces)


def chunk_of(place):
    return next(n for n, (low, high) in enumerate(CHUNKS) if low <= place < high)


def level_kernel(level, used, x_ref, table_ref, right_ref, *refs):
    places = PLACES[level]
    refs = list(refs)

    def take(count):
        taken = refs[:count]
        del refs[:count]
        return taken

    diag_refs = take(4)
    parts = {n: take(5 if FORWARD[n] else 4) for n in used}
    windows = take(4 * level)
    take(1)
    out_ref = take(1)[0]
    solved_ref = take(1)[0]
    window, window_sems, out_sems = refs
    columns = right_ref.shape[1]
    x_at = x_ref[0]
    begin, end = table_ref[8 + level], table_ref[12 + level]

    def block(place, k):
        n = chunk_of(place)
        low, high = CHUNKS[n]
        at, half = place - low, (high - low) // 2
        own, before, after = (ref[at, k] for ref in parts[n][:3])
        across = parts[n][3:]
        if not FORWARD[n]:
            last = across[0][at, k]
        elif high - low == 1:
            last = across[0][0, k] if k < 4 else across[1][0, k - 4]
        else:
            last = across[0][at, k] if at < half else across[1][at - half, k]
        return jnp.concatenate([before, own, after, last], axis=0)

    def store(place):
        at = pl.multiple_of((place - begin) * columns, columns)
        return pltpu.make_async_copy(
            solved_ref.at[pl.ds(at, columns)], out_ref.at[table_ref[place]], out_sems.at[place - places[0]]
        )

    incoming = [
        pltpu.make_async_copy(
            ref.at[pl.ds(0, CAP * columns)], window.at[pl.ds(n * CAP * columns, CAP * columns)], window_sems.at[n]
        )
        for n, ref in enumerate(windows)
    ]
    for copy in incoming:
        copy.start()
    for copy in incoming:
        copy.wait()
    for place in places:

        @pl.when((place >= begin) & (place < end))
        def _(place=place):
            row = table_ref[place]
            total = jnp.zeros(right_ref.shape[1:], jnp.float32)
            for k in range(8):
                at = pl.multiple_of(table_ref[16 + 8 * place + k] * columns, columns)
                total = total + dot_t(window[pl.ds(at, columns)], block(place, k))
            residue = (right_ref[row].astype(jnp.float32) - in_order(x_at, total)).astype(jnp.bfloat16)
            own, before, after, across = (ref[row] for ref in diag_refs)
            updated = dot_t(residue, jnp.concatenate([before, own, after, across], axis=0))
            at = pl.multiple_of((place - begin) * columns, columns)
            solved_ref[pl.ds(at, columns)] = in_order(x_at, updated).astype(solved_ref.dtype)
            store(place).start()

    for place in places:

        @pl.when((place >= begin) & (place < end))
        def _(place=place):
            store(place).wait()


def level_call(level, x_at, table, right, diag_pieces, parts, windows, out):
    rows, columns, size = right.shape
    places = PLACES[level]
    used = sorted({chunk_of(place) for place in places})
    flat = [piece for n in used for piece in parts[n]]
    operands = [x_at, table, right, *diag_pieces, *flat, *windows, out]
    count = len(places)
    return pl.pallas_call(
        functools.partial(level_kernel, level, used),
        out_shape=[
            jax.ShapeDtypeStruct(out.shape, out.dtype),
            jax.ShapeDtypeStruct((CAP * columns, size), out.dtype),
        ],
        in_specs=[SMEM, SMEM] + [VMEM] * (len(operands) - 3) + [ANY],
        out_specs=[ANY, VMEM],
        input_output_aliases={len(operands) - 1: 0},
        scratch_shapes=[
            pltpu.VMEM((4 * level * CAP * columns, size), out.dtype),
            pltpu.SemaphoreType.DMA((4 * level,)),
            pltpu.SemaphoreType.DMA((count,)),
        ],
        compiler_params=PARAMS,
        cost_estimate=pl.CostEstimate(
            flops=2 * CAP * 9 * columns * size * size, bytes_accessed=8 * 2**20, transcendentals=0
        ),
    )(*operands)


def round_x(block, distance):
    size = lax.axis_size("rhs")
    return lax.ppermute(block, "rhs", [(i, (i + distance) % size) for i in range(size)])


def up(block, distance):
    size = lax.axis_size("rows")
    return lax.ppermute(block, "rows", [(i, i + distance) for i in range(size - distance)])


def per_device(right, off, diag, level, columns):
    x_at = lax.axis_index("rhs").astype(jnp.int32).reshape(1)
    rows_at = lax.axis_index("rows").astype(jnp.int32).reshape(1)
    diag_pieces = [diag, round_x(diag, 1), round_x(diag, -1), round_x(diag, 2)]
    chunks = sort_call(level, off)
    parts = []
    for chunk, forward in zip(chunks, FORWARD):
        before, after = round_x(chunk, 1), round_x(chunk, -1)
        if not forward:
            across = [round_x(chunk, 2)]
        elif chunk.shape[0] == 1:
            across = [round_x(before[:, :4], 1), round_x(after[:, 4:], -1)]
        else:
            half = chunk.shape[0] // 2
            across = [round_x(before[:half], 1), round_x(after[half:], -1)]
        parts.append([chunk, before, after, *across])
    out, solved = first_call(x_at, level, right, diag_pieces)
    windows = [solved] + [up(solved, distance) for distance in range(1, REACH)]
    table = table_call(rows_at, level, columns, windows[1:])
    for level_now in range(1, LEVELS):
        out, solved = level_call(level_now, x_at, table, right, diag_pieces, parts, windows, out)
        if level_now < LEVELS - 1:
            windows += [solved] + [up(solved, distance) for distance in range(1, REACH)]
    return out


def solution(mesh):
    return jax.shard_map(
        per_device,
        mesh=mesh,
        in_specs=(
            P("rows", "rhs", None),
            P("rows", None, "rhs", None),
            P("rows", "rhs", None),
            P("rows"),
            P("rows", None),
        ),
        out_specs=P("rows", "rhs", None),
        check_vma=False,
    )
```

```python
import functools

import jax
import jax.numpy as jnp
from jax import lax
from jax.experimental import pallas as pl
from jax.experimental.pallas import tpu as pltpu
from jax.sharding import PartitionSpec as P

LEVELS = 4
REACH = 4
CAP = 4
ANY = pl.BlockSpec(memory_space=pl.ANY)
SMEM = pl.BlockSpec(memory_space=pltpu.SMEM)
VMEM = pl.BlockSpec(memory_space=pltpu.VMEM)
PARAMS = pltpu.CompilerParams(vmem_limit_bytes=58 * 2**20)

PLACES = {1: range(0, 4), 2: range(1, 6), 3: range(2, 7), 0: range(4, 8)}
CHUNKS = ((0, 2), (2, 4), (4, 6), (6, 7))
FORWARD = (1, -1, 1, -1)


def order_of(level_ref, order_ref):
    at = jnp.int32(0)
    starts = {}
    for level in (1, 2, 3, 0):
        starts[level] = at
        for row in range(8):
            here = level_ref[row] == level

            @pl.when(here)
            def _(at=at, row=row):
                order_ref[at] = jnp.int32(row)

            at = at + here.astype(jnp.int32)
    return starts


def sort_kernel(level_ref, off_ref, *refs):
    chunks, (order_ref, sems) = refs[: len(CHUNKS)], refs[len(CHUNKS) :]
    order_of(level_ref, order_ref)
    copies = []
    for chunk_ref, (low, high) in zip(chunks, CHUNKS):
        for place in range(low, high):
            copies.append(
                pltpu.make_async_copy(off_ref.at[order_ref[place]], chunk_ref.at[place - low], sems.at[place])
            )
    for copy in copies:
        copy.start()
    for copy in copies:
        copy.wait()


def sort_call(level, off):
    return pl.pallas_call(
        sort_kernel,
        out_shape=[jax.ShapeDtypeStruct((high - low,) + off.shape[1:], off.dtype) for low, high in CHUNKS],
        in_specs=[SMEM, ANY],
        out_specs=[VMEM] * len(CHUNKS),
        scratch_shapes=[pltpu.SMEM((8,), jnp.int32), pltpu.SemaphoreType.DMA((8,))],
        compiler_params=pltpu.CompilerParams(vmem_limit_bytes=60 * 2**20),
    )(level, off)


TABLE = 80
TAIL = 16


def table_kernel(rows_at_ref, x_ref, level_ref, columns_ref, one_ref, two_ref, three_ref, table_ref, slot_ref, levels_ref, near_ref, sem):
    parts = [
        ref[ref.shape[0] - TAIL :, :128].astype(jnp.float32).astype(jnp.int32)[:8] for ref in (one_ref, two_ref, three_ref)
    ]
    lane = lax.broadcasted_iota(jnp.int32, (8, 128), 0)
    levels_ref[...] = jnp.where(lane == 0, parts[0], jnp.where(lane == 1, parts[1], parts[2]))
    copy = pltpu.make_async_copy(levels_ref, near_ref, sem)
    copy.start()
    starts = order_of(level_ref, table_ref)
    ends = {1: starts[2], 2: starts[3], 3: starts[0], 0: jnp.int32(8)}
    for level in range(LEVELS):
        table_ref[8 + level] = starts[level]
        table_ref[12 + level] = ends[level]
    copy.wait()
    for buffer in range(REACH):
        seen = [jnp.int32(0)] * LEVELS
        for row in range(8):
            level = level_ref[row] if buffer == 0 else near_ref[buffer - 1, row] & 3
            rank = jnp.int32(0)
            for other in range(LEVELS):
                here = level == other
                rank = jnp.where(here, seen[other], rank)
                seen[other] = seen[other] + here.astype(jnp.int32)
            slot_ref[buffer * 8 + row] = 16 * jnp.minimum(level, 2) + 4 * buffer + jnp.minimum(rank, CAP - 1)
    base = rows_at_ref[0]
    table_ref[72] = x_ref[0]
    for place in range(7):
        row = table_ref[place]
        for k in range(8):
            column = columns_ref[row, k]
            distance = jnp.clip(base - lax.shift_right_logical(column, 3), 0, REACH - 1)
            buffer = jnp.where((base & distance & 1) == 1, 4 - distance, distance)
            table_ref[16 + 8 * place + k] = slot_ref[buffer * 8 + (column & 7)]


def table_call(rows_at, x_at, level, columns, received):
    return pl.pallas_call(
        table_kernel,
        out_shape=jax.ShapeDtypeStruct((TABLE,), jnp.int32),
        in_specs=[SMEM] * 4 + [VMEM] * 3,
        out_specs=SMEM,
        scratch_shapes=[
            pltpu.SMEM((32,), jnp.int32),
            pltpu.VMEM((8, 128), jnp.int32),
            pltpu.SMEM((8, 128), jnp.int32),
            pltpu.SemaphoreType.DMA,
        ],
        compiler_params=PARAMS,
        cost_estimate=pl.CostEstimate(flops=10**9, bytes_accessed=2**20, transcendentals=0),
    )(rows_at, x_at, level, columns, *received)


def dot_t(x, y):
    return lax.dot_general(x, y, (((1,), (1,)), ((), ())), preferred_element_type=jnp.float32)


def in_order(x_at, total):
    return pltpu.roll(total, lax.rem(x_at + 3, 4) * 64, 1)


def first_kernel(
    x_ref, level_ref, right_ref, own_ref, before_ref, after_ref, across_ref,
    out_ref, diag_ref, solved_ref,
    order_ref, inverse, right_buf, solved_buf, tail_buf, sems, right_sems, out_sems, diag_sem, tail_sem,
):
    x_at = x_ref[0]
    columns = right_ref.shape[1]
    pieces = [
        pltpu.make_async_copy(ref, inverse.at[:, pl.ds(pl.multiple_of(lax.rem(x_at + shift, 4) * 64, 64), 64)], sems.at[n])
        for n, (ref, shift) in enumerate(((own_ref, 0), (before_ref, 3), (after_ref, 1), (across_ref, 2)))
    ]
    for piece in pieces:
        piece.start()
    begin = order_of(level_ref, order_ref)[0]

    def fetch(place):
        return pltpu.make_async_copy(
            right_ref.at[order_ref[place]], right_buf.at[place - 4], right_sems.at[place - 4]
        )

    def stores(place):
        at = pl.multiple_of((place - begin) * columns, columns)
        source = solved_buf.at[place - 4]
        return [
            pltpu.make_async_copy(source, solved_ref.at[pl.ds(at, columns)], out_sems.at[place - 4, 0]),
            pltpu.make_async_copy(source, out_ref.at[order_ref[place]], out_sems.at[place - 4, 1]),
        ]

    for place in PLACES[0]:

        @pl.when(place >= begin)
        def _(place=place):
            fetch(place).start()

    lane = lax.broadcasted_iota(jnp.int32, (TAIL, 256), 1)
    tail = jnp.zeros((TAIL, 256), jnp.int32)
    for row in range(8):
        tail = jnp.where(lane == row, level_ref[row], tail)
    tail_buf[...] = tail.astype(jnp.float32).astype(tail_buf.dtype)
    levels = pltpu.make_async_copy(tail_buf, solved_ref.at[pl.ds(CAP * columns, TAIL)], tail_sem)
    levels.start()
    for piece in pieces:
        piece.wait()
    whole = pltpu.make_async_copy(inverse, diag_ref, diag_sem)
    whole.start()
    for place in PLACES[0]:

        @pl.when(place >= begin)
        def _(place=place):
            fetch(place).wait()
            solved_buf[place - 4] = dot_t(right_buf[place - 4], inverse[order_ref[place]]).astype(solved_buf.dtype)
            for copy in stores(place):
                copy.start()

    for place in PLACES[0]:

        @pl.when(place >= begin)
        def _(place=place):
            for copy in stores(place):
                copy.wait()

    levels.wait()
    whole.wait()


def first_call(x_at, level, right, diag_pieces):
    rows, columns, size = right.shape
    return pl.pallas_call(
        first_kernel,
        out_shape=[
            jax.ShapeDtypeStruct(right.shape, right.dtype),
            jax.ShapeDtypeStruct((rows, size, size), right.dtype),
            jax.ShapeDtypeStruct((CAP * columns + TAIL, size), right.dtype),
        ],
        in_specs=[SMEM, SMEM] + [ANY] * 5,
        out_specs=[ANY, ANY, ANY],
        scratch_shapes=[
            pltpu.SMEM((8,), jnp.int32),
            pltpu.VMEM((rows, size, size), right.dtype),
            pltpu.VMEM((CAP, columns, size), right.dtype),
            pltpu.VMEM((CAP, columns, size), right.dtype),
            pltpu.VMEM((TAIL, size), right.dtype),
            pltpu.SemaphoreType.DMA((4,)),
            pltpu.SemaphoreType.DMA((CAP,)),
            pltpu.SemaphoreType.DMA((CAP, 2)),
            pltpu.SemaphoreType.DMA,
            pltpu.SemaphoreType.DMA,
        ],
        compiler_params=PARAMS,
        cost_estimate=pl.CostEstimate(flops=2 * CAP * columns * size * size, bytes_accessed=3 * 2**20, transcendentals=0),
    )(x_at, level, right, *diag_pieces)


def chunk_of(place):
    return next(n for n, (low, high) in enumerate(CHUNKS) if low <= place < high)


def level_kernel(level, used, table_ref, right_ref, diag_ref, *refs):
    places = PLACES[level]
    refs = list(refs)

    def take(count):
        taken = refs[:count]
        del refs[:count]
        return taken

    parts = {n: take(4) for n in used}
    windows = take(4 * level)
    take(1)
    out_ref = take(1)[0]
    solved_ref = take(1)[0] if level < LEVELS - 1 else None
    window, factor, diag_buf, right_buf, solved_buf, window_sems, factor_sems, row_sems, out_sems = refs
    columns = right_ref.shape[1]
    x_at = table_ref[72]
    begin, end = table_ref[8 + level], table_ref[12 + level]

    def fetches(place):
        slot = place - places[0]
        row = table_ref[place]
        copies = [
            pltpu.make_async_copy(right_ref.at[row], right_buf.at[slot], row_sems.at[slot, 0]),
            pltpu.make_async_copy(diag_ref.at[row], diag_buf.at[slot], row_sems.at[slot, 1]),
        ]
        n = chunk_of(place)
        for quarter, ref in enumerate(parts[n]):
            source = ref.at[place - CHUNKS[n][0]]
            copies.append(pltpu.make_async_copy(source, factor.at[slot, quarter], factor_sems.at[slot, quarter]))
        return copies

    def block(place, k):
        own, before, after, across = (factor[place - places[0], quarter, k] for quarter in range(4))
        return jnp.concatenate([before, own, after, across], axis=0)

    def stores(place):
        slot = place - places[0]
        copies = [pltpu.make_async_copy(solved_buf.at[slot], out_ref.at[table_ref[place]], out_sems.at[slot, 0])]
        if solved_ref is not None:
            at = pl.multiple_of((place - begin) * columns, columns)
            copies.append(
                pltpu.make_async_copy(solved_buf.at[slot], solved_ref.at[pl.ds(at, columns)], out_sems.at[slot, 1])
            )
        return copies

    incoming = [
        pltpu.make_async_copy(
            ref.at[pl.ds(0, CAP * columns)], window.at[pl.ds(n * CAP * columns, CAP * columns)], window_sems.at[n]
        )
        for n, ref in enumerate(windows)
    ]
    for copy in incoming:
        copy.start()
    for place in places:

        @pl.when((place >= begin) & (place < end))
        def _(place=place):
            for copy in fetches(place):
                copy.start()

    for copy in incoming:
        copy.wait()
    for place in places:

        @pl.when((place >= begin) & (place < end))
        def _(place=place):
            slot = place - places[0]
            for copy in fetches(place):
                copy.wait()
            total = jnp.zeros(right_buf.shape[1:], jnp.float32)
            for k in range(8):
                at = pl.multiple_of(table_ref[16 + 8 * place + k] * columns, columns)
                total = total + dot_t(window[pl.ds(at, columns)], block(place, k))
            residue = (right_buf[slot].astype(jnp.float32) - in_order(x_at, total)).astype(jnp.bfloat16)
            solved_buf[slot] = dot_t(residue, diag_buf[slot]).astype(solved_buf.dtype)
            for copy in stores(place):
                copy.start()

    for place in places:

        @pl.when((place >= begin) & (place < end))
        def _(place=place):
            for copy in stores(place):
                copy.wait()


def level_call(level, table, right, diag, parts, windows, out):
    rows, columns, size = right.shape
    places = PLACES[level]
    used = sorted({chunk_of(place) for place in places})
    flat = [piece for n in used for piece in parts[n]]
    operands = [table, right, diag, *flat, *windows, out]
    count = len(places)
    return pl.pallas_call(
        functools.partial(level_kernel, level, used),
        out_shape=[
            jax.ShapeDtypeStruct(out.shape, out.dtype),
            jax.ShapeDtypeStruct((CAP * columns, size), out.dtype),
        ][: 1 if level == LEVELS - 1 else 2],
        in_specs=[SMEM] + [ANY] * (len(operands) - 1),
        out_specs=[ANY, ANY][: 1 if level == LEVELS - 1 else 2],
        input_output_aliases={len(operands) - 1: 0},
        scratch_shapes=[
            pltpu.VMEM((4 * level * CAP * columns, size), out.dtype),
            pltpu.VMEM((count, 4, 8, size // 4, size), out.dtype),
            pltpu.VMEM((count, size, size), out.dtype),
            pltpu.VMEM((count, columns, size), out.dtype),
            pltpu.VMEM((count, columns, size), out.dtype),
            pltpu.SemaphoreType.DMA((4 * level,)),
            pltpu.SemaphoreType.DMA((count, 4)),
            pltpu.SemaphoreType.DMA((count, 2)),
            pltpu.SemaphoreType.DMA((count, 2)),
        ],
        compiler_params=PARAMS,
        cost_estimate=pl.CostEstimate(
            flops=2 * CAP * 9 * columns * size * size, bytes_accessed=8 * 2**20, transcendentals=0
        ),
    )(*operands)


def round_x(block, distance):
    size = lax.axis_size("rhs")
    return lax.ppermute(block, "rhs", [(i, (i + distance) % size) for i in range(size)])


def up(block, distance):
    size = lax.axis_size("rows")
    return lax.ppermute(block, "rows", [(i, i + distance) for i in range(size - distance)])


def after(value, *others):
    return lax.optimization_barrier((value, others))[0]


def ring(chunk, forward, *before):
    low, high = round_x(chunk, 1), round_x(chunk, -1)
    if forward == 0:
        return [chunk, low, high, round_x(chunk, 2)]
    return [chunk, low, high, round_x(after(low if forward > 0 else high, *before), forward)]


def shift(solved):
    size = lax.axis_size("rows")
    two = up(solved, 2)
    mixed = lax.ppermute(
        solved, "rows", [(i, i + (3 if i % 2 else 1)) for i in range(size) if i + (3 if i % 2 else 1) < size]
    )
    swapped = lax.ppermute(after(two, mixed), "rows", [(i, i ^ 1) for i in range(size)])
    return [solved, swapped, two, mixed]


def per_device(right, off, diag, level, columns):
    x_at = lax.axis_index("rhs").astype(jnp.int32).reshape(1)
    rows_at = lax.axis_index("rows").astype(jnp.int32).reshape(1)
    diag_pieces = ring(diag, 0)
    chunks = sort_call(level, off)
    out, diag, solved = first_call(x_at, level, right, diag_pieces)
    windows = shift(solved)
    parts = [ring(chunks[0], FORWARD[0], solved), ring(after(chunks[1], *diag_pieces), FORWARD[1], solved)]
    table = table_call(rows_at, x_at, level, columns, windows[1:])
    parts.append(ring(after(chunks[2], *parts[1], *parts[0], table), FORWARD[2]))
    out, solved = level_call(1, table, right, diag, parts, windows, out)
    windows += shift(solved)
    parts.append(ring(after(chunks[3], *parts[2][:3]), FORWARD[3]))
    out, solved = level_call(2, table, right, diag, parts, windows, out)
    windows += shift(solved)
    return level_call(3, table, right, diag, parts, windows, out)[0]


def solution(mesh):
    return jax.shard_map(
        per_device,
        mesh=mesh,
        in_specs=(
            P("rows", "rhs", None),
            P("rows", None, "rhs", None),
            P("rows", "rhs", None),
            P("rows"),
            P("rows", None),
        ),
        out_specs=P("rows", "rhs", None),
        check_vma=False,
    )
```

```python
import functools

import jax
import jax.numpy as jnp
from jax import lax
from jax.experimental import pallas as pl
from jax.experimental.pallas import tpu as pltpu
from jax.sharding import PartitionSpec as P

LEVELS = 4
REACH = 4
CAP = 4
ANY = pl.BlockSpec(memory_space=pl.ANY)
SMEM = pl.BlockSpec(memory_space=pltpu.SMEM)
VMEM = pl.BlockSpec(memory_space=pltpu.VMEM)
PARAMS = pltpu.CompilerParams(vmem_limit_bytes=58 * 2**20)

PLACES = {1: range(0, 4), 2: range(1, 6), 3: range(2, 7), 0: range(4, 8)}
CHUNKS = ((0, 2), (2, 4), (4, 6), (6, 7))
FORWARD = (1, -1, 1, -1)


def order_of(level_ref, order_ref):
    at = jnp.int32(0)
    starts = {}
    for level in (1, 2, 3, 0):
        starts[level] = at
        for row in range(8):
            here = level_ref[row] == level

            @pl.when(here)
            def _(at=at, row=row):
                order_ref[at] = jnp.int32(row)

            at = at + here.astype(jnp.int32)
    return starts


def sort_kernel(level_ref, off_ref, *refs):
    chunks, (order_ref, sems) = refs[: len(CHUNKS)], refs[len(CHUNKS) :]
    order_of(level_ref, order_ref)
    copies = []
    for chunk_ref, (low, high) in zip(chunks, CHUNKS):
        for place in range(low, high):
            copies.append(
                pltpu.make_async_copy(off_ref.at[order_ref[place]], chunk_ref.at[place - low], sems.at[place])
            )
    for copy in copies:
        copy.start()
    for copy in copies:
        copy.wait()


def sort_call(level, off):
    return pl.pallas_call(
        sort_kernel,
        out_shape=[jax.ShapeDtypeStruct((high - low,) + off.shape[1:], off.dtype) for low, high in CHUNKS],
        in_specs=[SMEM, ANY],
        out_specs=[VMEM] * len(CHUNKS),
        scratch_shapes=[pltpu.SMEM((8,), jnp.int32), pltpu.SemaphoreType.DMA((8,))],
        compiler_params=pltpu.CompilerParams(vmem_limit_bytes=60 * 2**20),
    )(level, off)


TABLE = 80
TAIL = 16


def table_kernel(rows_at_ref, x_ref, level_ref, columns_ref, one_ref, two_ref, three_ref, table_ref, slot_ref, levels_ref, near_ref, sem):
    parts = [
        ref[ref.shape[0] - TAIL :, :128].astype(jnp.float32).astype(jnp.int32)[:8] for ref in (one_ref, two_ref, three_ref)
    ]
    lane = lax.broadcasted_iota(jnp.int32, (8, 128), 0)
    levels_ref[...] = jnp.where(lane == 0, parts[0], jnp.where(lane == 1, parts[1], parts[2]))
    copy = pltpu.make_async_copy(levels_ref, near_ref, sem)
    copy.start()
    starts = order_of(level_ref, table_ref)
    ends = {1: starts[2], 2: starts[3], 3: starts[0], 0: jnp.int32(8)}
    for level in range(LEVELS):
        table_ref[8 + level] = starts[level]
        table_ref[12 + level] = ends[level]
    copy.wait()
    for buffer in range(REACH):
        seen = [jnp.int32(0)] * LEVELS
        for row in range(8):
            level = level_ref[row] if buffer == 0 else near_ref[buffer - 1, row] & 3
            rank = jnp.int32(0)
            for other in range(LEVELS):
                here = level == other
                rank = jnp.where(here, seen[other], rank)
                seen[other] = seen[other] + here.astype(jnp.int32)
            slot_ref[buffer * 8 + row] = 16 * jnp.minimum(level, 2) + 4 * buffer + jnp.minimum(rank, CAP - 1)
    base = rows_at_ref[0]
    table_ref[72] = x_ref[0]
    for place in range(7):
        row = table_ref[place]
        for k in range(8):
            column = columns_ref[row, k]
            distance = jnp.clip(base - lax.shift_right_logical(column, 3), 0, REACH - 1)
            buffer = jnp.where((base & distance & 1) == 1, 4 - distance, distance)
            table_ref[16 + 8 * place + k] = slot_ref[buffer * 8 + (column & 7)]


def table_call(rows_at, x_at, level, columns, received):
    return pl.pallas_call(
        table_kernel,
        out_shape=jax.ShapeDtypeStruct((TABLE,), jnp.int32),
        in_specs=[SMEM] * 4 + [VMEM] * 3,
        out_specs=SMEM,
        scratch_shapes=[
            pltpu.SMEM((32,), jnp.int32),
            pltpu.VMEM((8, 128), jnp.int32),
            pltpu.SMEM((8, 128), jnp.int32),
            pltpu.SemaphoreType.DMA,
        ],
        compiler_params=PARAMS,
        cost_estimate=pl.CostEstimate(flops=10**9, bytes_accessed=2**20, transcendentals=0),
    )(rows_at, x_at, level, columns, *received)


def dot_t(x, y):
    return lax.dot_general(x, y, (((1,), (1,)), ((), ())), preferred_element_type=jnp.float32)


def first_kernel(
    x_ref, level_ref, right_ref, own_ref, before_ref, after_ref, across_ref,
    out_ref, diag_ref, solved_ref,
    order_ref, inverse, right_buf, solved_buf, tail_buf, sems, right_sems, out_sems, diag_sem, tail_sem,
):
    x_at = x_ref[0]
    columns = right_ref.shape[1]
    pieces = [
        pltpu.make_async_copy(ref, inverse.at[:, pl.ds(pl.multiple_of(lax.rem(x_at + shift, 4) * 64, 64), 64)], sems.at[n])
        for n, (ref, shift) in enumerate(((own_ref, 0), (before_ref, 3), (after_ref, 1), (across_ref, 2)))
    ]
    for piece in pieces:
        piece.start()
    begin = order_of(level_ref, order_ref)[0]

    def fetch(place):
        return pltpu.make_async_copy(
            right_ref.at[order_ref[place]], right_buf.at[place - 4], right_sems.at[place - 4]
        )

    def stores(place):
        at = pl.multiple_of((place - begin) * columns, columns)
        source = solved_buf.at[place - 4]
        return [
            pltpu.make_async_copy(source, solved_ref.at[pl.ds(at, columns)], out_sems.at[place - 4, 0]),
            pltpu.make_async_copy(source, out_ref.at[order_ref[place]], out_sems.at[place - 4, 1]),
        ]

    for place in PLACES[0]:

        @pl.when(place >= begin)
        def _(place=place):
            fetch(place).start()

    lane = lax.broadcasted_iota(jnp.int32, (TAIL, 256), 1)
    tail = jnp.zeros((TAIL, 256), jnp.int32)
    for row in range(8):
        tail = jnp.where(lane == row, level_ref[row], tail)
    tail_buf[...] = tail.astype(jnp.float32).astype(tail_buf.dtype)
    levels = pltpu.make_async_copy(tail_buf, solved_ref.at[pl.ds(CAP * columns, TAIL)], tail_sem)
    levels.start()
    for piece in pieces:
        piece.wait()
    whole = pltpu.make_async_copy(inverse, diag_ref, diag_sem)
    whole.start()
    for place in PLACES[0]:

        @pl.when(place >= begin)
        def _(place=place):
            fetch(place).wait()
            solved_buf[place - 4] = dot_t(right_buf[place - 4], inverse[order_ref[place]]).astype(solved_buf.dtype)
            for copy in stores(place):
                copy.start()

    for place in PLACES[0]:

        @pl.when(place >= begin)
        def _(place=place):
            for copy in stores(place):
                copy.wait()

    levels.wait()
    whole.wait()


def first_call(x_at, level, right, diag_pieces):
    rows, columns, size = right.shape
    return pl.pallas_call(
        first_kernel,
        out_shape=[
            jax.ShapeDtypeStruct(right.shape, right.dtype),
            jax.ShapeDtypeStruct((rows, size, size), right.dtype),
            jax.ShapeDtypeStruct((CAP * columns + TAIL, size), right.dtype),
        ],
        in_specs=[SMEM, SMEM] + [ANY] * 5,
        out_specs=[ANY, ANY, ANY],
        scratch_shapes=[
            pltpu.SMEM((8,), jnp.int32),
            pltpu.VMEM((rows, size, size), right.dtype),
            pltpu.VMEM((CAP, columns, size), right.dtype),
            pltpu.VMEM((CAP, columns, size), right.dtype),
            pltpu.VMEM((TAIL, size), right.dtype),
            pltpu.SemaphoreType.DMA((4,)),
            pltpu.SemaphoreType.DMA((CAP,)),
            pltpu.SemaphoreType.DMA((CAP, 2)),
            pltpu.SemaphoreType.DMA,
            pltpu.SemaphoreType.DMA,
        ],
        compiler_params=PARAMS,
        cost_estimate=pl.CostEstimate(flops=2 * CAP * columns * size * size, bytes_accessed=3 * 2**20, transcendentals=0),
    )(x_at, level, right, *diag_pieces)


def chunk_of(place):
    return next(n for n, (low, high) in enumerate(CHUNKS) if low <= place < high)


def level_kernel(level, used, table_ref, right_ref, diag_ref, *refs):
    places = PLACES[level]
    refs = list(refs)

    def take(count):
        taken = refs[:count]
        del refs[:count]
        return taken

    parts = {n: take(4) for n in used}
    windows = take(4 * level)
    take(1)
    out_ref = take(1)[0]
    solved_ref = take(1)[0] if level < LEVELS - 1 else None
    window, factor, diag_buf, right_buf, solved_buf, totals, window_sems, factor_sems, row_sems, out_sems = refs
    columns = right_ref.shape[1]
    x_at = table_ref[72]
    begin, end = table_ref[8 + level], table_ref[12 + level]

    def fetches(place):
        slot = place - places[0]
        row = table_ref[place]
        copies = [
            pltpu.make_async_copy(right_ref.at[row], right_buf.at[slot], row_sems.at[slot, 0]),
            pltpu.make_async_copy(diag_ref.at[row], diag_buf.at[slot], row_sems.at[slot, 1]),
        ]
        n = chunk_of(place)
        for quarter, (ref, turn) in enumerate(zip(parts[n], (0, 3, 1, 2))):
            source = ref.at[place - CHUNKS[n][0]]
            target = factor.at[slot, :, pl.ds(pl.multiple_of(lax.rem(x_at + turn, 4) * 64, 64), 64), :]
            copies.append(pltpu.make_async_copy(source, target, factor_sems.at[slot, quarter]))
        return copies

    def stores(place):
        slot = place - places[0]
        copies = [pltpu.make_async_copy(solved_buf.at[slot], out_ref.at[table_ref[place]], out_sems.at[slot, 0])]
        if solved_ref is not None:
            at = pl.multiple_of((place - begin) * columns, columns)
            copies.append(
                pltpu.make_async_copy(solved_buf.at[slot], solved_ref.at[pl.ds(at, columns)], out_sems.at[slot, 1])
            )
        return copies

    incoming = [
        pltpu.make_async_copy(
            ref.at[pl.ds(0, CAP * columns)], window.at[pl.ds(n * CAP * columns, CAP * columns)], window_sems.at[n]
        )
        for n, ref in enumerate(windows)
    ]
    for copy in incoming:
        copy.start()
    for place in places:

        @pl.when((place >= begin) & (place < end))
        def _(place=place):
            for copy in fetches(place):
                copy.start()

    for copy in incoming:
        copy.wait()
    for place in places:

        @pl.when((place >= begin) & (place < end))
        def _(place=place):
            slot = place - places[0]
            for copy in fetches(place):
                copy.wait()
            total = jnp.zeros(right_buf.shape[1:], jnp.float32)
            for k in range(8):
                at = pl.multiple_of(table_ref[16 + 8 * place + k] * columns, columns)
                total = total + dot_t(window[pl.ds(at, columns)], factor[slot, k])
            totals[slot] = total

    for place in places:
        slot = place - places[0]
        residue = (right_buf[slot].astype(jnp.float32) - totals[slot]).astype(jnp.bfloat16)
        solved_buf[slot] = dot_t(residue, diag_buf[slot]).astype(solved_buf.dtype)
    for place in places:

        @pl.when((place >= begin) & (place < end))
        def _(place=place):
            for copy in stores(place):
                copy.start()

    for place in places:

        @pl.when((place >= begin) & (place < end))
        def _(place=place):
            for copy in stores(place):
                copy.wait()


def level_call(level, table, right, diag, parts, windows, out):
    rows, columns, size = right.shape
    places = PLACES[level]
    used = sorted({chunk_of(place) for place in places})
    flat = [piece for n in used for piece in parts[n]]
    operands = [table, right, diag, *flat, *windows, out]
    count = len(places)
    return pl.pallas_call(
        functools.partial(level_kernel, level, used),
        out_shape=[
            jax.ShapeDtypeStruct(out.shape, out.dtype),
            jax.ShapeDtypeStruct((CAP * columns, size), out.dtype),
        ][: 1 if level == LEVELS - 1 else 2],
        in_specs=[SMEM] + [ANY] * (len(operands) - 1),
        out_specs=[ANY, ANY][: 1 if level == LEVELS - 1 else 2],
        input_output_aliases={len(operands) - 1: 0},
        scratch_shapes=[
            pltpu.VMEM((4 * level * CAP * columns, size), out.dtype),
            pltpu.VMEM((count, 8, size, size), out.dtype),
            pltpu.VMEM((count, size, size), out.dtype),
            pltpu.VMEM((count, columns, size), out.dtype),
            pltpu.VMEM((count, columns, size), out.dtype),
            pltpu.VMEM((count, columns, size), jnp.float32),
            pltpu.SemaphoreType.DMA((4 * level,)),
            pltpu.SemaphoreType.DMA((count, 4)),
            pltpu.SemaphoreType.DMA((count, 2)),
            pltpu.SemaphoreType.DMA((count, 2)),
        ],
        compiler_params=PARAMS,
        cost_estimate=pl.CostEstimate(
            flops=2 * CAP * 9 * columns * size * size, bytes_accessed=8 * 2**20, transcendentals=0
        ),
    )(*operands)


def round_x(block, distance):
    size = lax.axis_size("rhs")
    return lax.ppermute(block, "rhs", [(i, (i + distance) % size) for i in range(size)])


def up(block, distance):
    size = lax.axis_size("rows")
    return lax.ppermute(block, "rows", [(i, i + distance) for i in range(size - distance)])


def after(value, *others):
    return lax.optimization_barrier((value, others))[0]


def ring(chunk, forward, *before):
    low, high = round_x(chunk, 1), round_x(chunk, -1)
    if forward == 0:
        return [chunk, low, high, round_x(chunk, 2)]
    return [chunk, low, high, round_x(after(low if forward > 0 else high, *before), forward)]


def shift(solved):
    size = lax.axis_size("rows")
    two = up(solved, 2)
    mixed = lax.ppermute(
        solved, "rows", [(i, i + (3 if i % 2 else 1)) for i in range(size) if i + (3 if i % 2 else 1) < size]
    )
    swapped = lax.ppermute(after(two, mixed), "rows", [(i, i ^ 1) for i in range(size)])
    return [solved, swapped, two, mixed]


def per_device(right, off, diag, level, columns):
    x_at = lax.axis_index("rhs").astype(jnp.int32).reshape(1)
    rows_at = lax.axis_index("rows").astype(jnp.int32).reshape(1)
    diag_pieces = ring(diag, 0)
    chunks = sort_call(level, off)
    out, diag, solved = first_call(x_at, level, right, diag_pieces)
    windows = shift(solved)
    parts = []
    for chunk, ahead in ((chunks[0], []), (chunks[1], [*diag_pieces])):
        chunk = after(chunk, *ahead)
        parts.append([chunk, round_x(chunk, 1), round_x(chunk, -1)])
    ahead = [solved, *parts[0], *parts[1]]
    parts[0].append(round_x(after(parts[0][1], solved), 1))
    parts[1].append(round_x(after(parts[1][2], *ahead), -1))
    table = table_call(rows_at, x_at, level, columns, windows[1:])
    parts.append(ring(after(chunks[2], *parts[1], *parts[0], table), FORWARD[2]))
    out, solved = level_call(1, table, right, diag, parts, windows, out)
    windows += shift(solved)
    parts.append(ring(after(chunks[3], *parts[2][:3]), FORWARD[3]))
    out, solved = level_call(2, table, right, diag, parts, windows, out)
    windows += shift(solved)
    return level_call(3, table, right, diag, parts, windows, out)[0]


def solution(mesh):
    return jax.shard_map(
        per_device,
        mesh=mesh,
        in_specs=(
            P("rows", "rhs", None),
            P("rows", None, "rhs", None),
            P("rows", "rhs", None),
            P("rows"),
            P("rows", None),
        ),
        out_specs=P("rows", "rhs", None),
        check_vma=False,
    )
```

```python
import functools

import jax
import jax.numpy as jnp
from jax import lax
from jax.experimental import pallas as pl
from jax.experimental.pallas import tpu as pltpu
from jax.sharding import PartitionSpec as P

LEVELS = 4
REACH = 4
CAP = 4
ANY = pl.BlockSpec(memory_space=pl.ANY)
SMEM = pl.BlockSpec(memory_space=pltpu.SMEM)
VMEM = pl.BlockSpec(memory_space=pltpu.VMEM)
PARAMS = pltpu.CompilerParams(vmem_limit_bytes=58 * 2**20)

PLACES = {1: range(0, 4), 2: range(1, 6), 3: range(2, 7), 0: range(4, 8)}
CHUNKS = ((0, 2), (2, 4), (4, 6), (6, 7))
FORWARD = (1, -1, 1, -1)


def order_of(level_ref, order_ref):
    at = jnp.int32(0)
    starts = {}
    for level in (1, 2, 3, 0):
        starts[level] = at
        for row in range(8):
            here = level_ref[row] == level

            @pl.when(here)
            def _(at=at, row=row):
                order_ref[at] = jnp.int32(row)

            at = at + here.astype(jnp.int32)
    return starts


def sort_kernel(level_ref, off_ref, *refs):
    chunks, (order_ref, sems) = refs[: len(CHUNKS)], refs[len(CHUNKS) :]
    order_of(level_ref, order_ref)
    copies = []
    for chunk_ref, (low, high) in zip(chunks, CHUNKS):
        for place in range(low, high):
            copies.append(
                pltpu.make_async_copy(off_ref.at[order_ref[place]], chunk_ref.at[place - low], sems.at[place])
            )
    for copy in copies:
        copy.start()
    for copy in copies:
        copy.wait()


def sort_call(level, off):
    return pl.pallas_call(
        sort_kernel,
        out_shape=[jax.ShapeDtypeStruct((high - low,) + off.shape[1:], off.dtype) for low, high in CHUNKS],
        in_specs=[SMEM, ANY],
        out_specs=[VMEM] * len(CHUNKS),
        scratch_shapes=[pltpu.SMEM((8,), jnp.int32), pltpu.SemaphoreType.DMA((8,))],
        compiler_params=pltpu.CompilerParams(vmem_limit_bytes=60 * 2**20),
    )(level, off)


TABLE = 80
TAIL = 16


def table_kernel(rows_at_ref, x_ref, level_ref, columns_ref, one_ref, two_ref, three_ref, table_ref, slot_ref, levels_ref, near_ref, sem):
    parts = [
        ref[ref.shape[0] - TAIL :, :128].astype(jnp.float32).astype(jnp.int32)[:8] for ref in (one_ref, two_ref, three_ref)
    ]
    lane = lax.broadcasted_iota(jnp.int32, (8, 128), 0)
    levels_ref[...] = jnp.where(lane == 0, parts[0], jnp.where(lane == 1, parts[1], parts[2]))
    copy = pltpu.make_async_copy(levels_ref, near_ref, sem)
    copy.start()
    starts = order_of(level_ref, table_ref)
    ends = {1: starts[2], 2: starts[3], 3: starts[0], 0: jnp.int32(8)}
    for level in range(LEVELS):
        table_ref[8 + level] = starts[level]
        table_ref[12 + level] = ends[level]
    copy.wait()
    for buffer in range(REACH):
        seen = [jnp.int32(0)] * LEVELS
        for row in range(8):
            level = level_ref[row] if buffer == 0 else near_ref[buffer - 1, row] & 3
            rank = jnp.int32(0)
            for other in range(LEVELS):
                here = level == other
                rank = jnp.where(here, seen[other], rank)
                seen[other] = seen[other] + here.astype(jnp.int32)
            slot_ref[buffer * 8 + row] = 16 * jnp.minimum(level, 2) + 4 * buffer + jnp.minimum(rank, CAP - 1)
    base = rows_at_ref[0]
    table_ref[72] = x_ref[0]
    for place in range(7):
        row = table_ref[place]
        for k in range(8):
            column = columns_ref[row, k]
            distance = jnp.clip(base - lax.shift_right_logical(column, 3), 0, REACH - 1)
            buffer = jnp.where((base & distance & 1) == 1, 4 - distance, distance)
            table_ref[16 + 8 * place + k] = slot_ref[buffer * 8 + (column & 7)]


def table_call(rows_at, x_at, level, columns, received):
    return pl.pallas_call(
        table_kernel,
        out_shape=jax.ShapeDtypeStruct((TABLE,), jnp.int32),
        in_specs=[SMEM] * 4 + [VMEM] * 3,
        out_specs=SMEM,
        scratch_shapes=[
            pltpu.SMEM((32,), jnp.int32),
            pltpu.VMEM((8, 128), jnp.int32),
            pltpu.SMEM((8, 128), jnp.int32),
            pltpu.SemaphoreType.DMA,
        ],
        compiler_params=PARAMS,
        cost_estimate=pl.CostEstimate(flops=10**9, bytes_accessed=2**20, transcendentals=0),
    )(rows_at, x_at, level, columns, *received)


def dot_t(x, y):
    return lax.dot_general(x, y, (((1,), (1,)), ((), ())), preferred_element_type=jnp.float32)


def first_kernel(
    x_ref, level_ref, right_ref, own_ref, before_ref, after_ref, low_ref, high_ref,
    out_ref, diag_ref, solved_ref,
    order_ref, inverse, right_buf, solved_buf, tail_buf, sems, right_sems, out_sems, diag_sem, tail_sem,
):
    x_at = x_ref[0]
    columns = right_ref.shape[1]
    half = low_ref.shape[0]
    whole, low, high = pl.ds(0, 2 * half), pl.ds(0, half), pl.ds(half, half)
    sources = ((own_ref, 0, whole), (before_ref, 3, whole), (after_ref, 1, whole), (low_ref, 2, low), (high_ref, 2, high))
    pieces = []
    for n, (ref, turn, rows) in enumerate(sources):
        at = pl.multiple_of(lax.rem(x_at + turn, 4) * 64, 64)
        pieces.append(pltpu.make_async_copy(ref, inverse.at[rows, pl.ds(at, 64)], sems.at[n]))
    for piece in pieces:
        piece.start()
    begin = order_of(level_ref, order_ref)[0]

    def fetch(place):
        return pltpu.make_async_copy(
            right_ref.at[order_ref[place]], right_buf.at[place - 4], right_sems.at[place - 4]
        )

    def stores(place):
        at = pl.multiple_of((place - begin) * columns, columns)
        source = solved_buf.at[place - 4]
        return [
            pltpu.make_async_copy(source, solved_ref.at[pl.ds(at, columns)], out_sems.at[place - 4, 0]),
            pltpu.make_async_copy(source, out_ref.at[order_ref[place]], out_sems.at[place - 4, 1]),
        ]

    for place in PLACES[0]:

        @pl.when(place >= begin)
        def _(place=place):
            fetch(place).start()

    lane = lax.broadcasted_iota(jnp.int32, (TAIL, 256), 1)
    tail = jnp.zeros((TAIL, 256), jnp.int32)
    for row in range(8):
        tail = jnp.where(lane == row, level_ref[row], tail)
    tail_buf[...] = tail.astype(jnp.float32).astype(tail_buf.dtype)
    levels = pltpu.make_async_copy(tail_buf, solved_ref.at[pl.ds(CAP * columns, TAIL)], tail_sem)
    levels.start()
    for piece in pieces:
        piece.wait()
    whole = pltpu.make_async_copy(inverse, diag_ref, diag_sem)
    whole.start()
    for place in PLACES[0]:

        @pl.when(place >= begin)
        def _(place=place):
            fetch(place).wait()
            solved_buf[place - 4] = dot_t(right_buf[place - 4], inverse[order_ref[place]]).astype(solved_buf.dtype)
            for copy in stores(place):
                copy.start()

    for place in PLACES[0]:

        @pl.when(place >= begin)
        def _(place=place):
            for copy in stores(place):
                copy.wait()

    levels.wait()
    whole.wait()


def first_call(x_at, level, right, diag_pieces):
    rows, columns, size = right.shape
    return pl.pallas_call(
        first_kernel,
        out_shape=[
            jax.ShapeDtypeStruct(right.shape, right.dtype),
            jax.ShapeDtypeStruct((rows, size, size), right.dtype),
            jax.ShapeDtypeStruct((CAP * columns + TAIL, size), right.dtype),
        ],
        in_specs=[SMEM, SMEM] + [ANY] * 6,
        out_specs=[ANY, ANY, ANY],
        scratch_shapes=[
            pltpu.SMEM((8,), jnp.int32),
            pltpu.VMEM((rows, size, size), right.dtype),
            pltpu.VMEM((CAP, columns, size), right.dtype),
            pltpu.VMEM((CAP, columns, size), right.dtype),
            pltpu.VMEM((TAIL, size), right.dtype),
            pltpu.SemaphoreType.DMA((5,)),
            pltpu.SemaphoreType.DMA((CAP,)),
            pltpu.SemaphoreType.DMA((CAP, 2)),
            pltpu.SemaphoreType.DMA,
            pltpu.SemaphoreType.DMA,
        ],
        compiler_params=PARAMS,
        cost_estimate=pl.CostEstimate(flops=2 * CAP * columns * size * size, bytes_accessed=3 * 2**20, transcendentals=0),
    )(x_at, level, right, *diag_pieces)


def chunk_of(place):
    return next(n for n, (low, high) in enumerate(CHUNKS) if low <= place < high)


def level_kernel(level, used, table_ref, right_ref, diag_ref, *refs):
    places = PLACES[level]
    refs = list(refs)

    def take(count):
        taken = refs[:count]
        del refs[:count]
        return taken

    parts = {n: take(4) for n in used}
    windows = take(4 * level)
    take(1)
    out_ref = take(1)[0]
    solved_ref = take(1)[0] if level < LEVELS - 1 else None
    window, factor, diag_buf, right_buf, solved_buf, totals, window_sems, factor_sems, row_sems, out_sems = refs
    columns = right_ref.shape[1]
    x_at = table_ref[72]
    begin, end = table_ref[8 + level], table_ref[12 + level]

    def fetches(place):
        slot = place - places[0]
        row = table_ref[place]
        copies = [
            pltpu.make_async_copy(right_ref.at[row], right_buf.at[slot], row_sems.at[slot, 0]),
            pltpu.make_async_copy(diag_ref.at[row], diag_buf.at[slot], row_sems.at[slot, 1]),
        ]
        n = chunk_of(place)
        for quarter, (ref, turn) in enumerate(zip(parts[n], (0, 3, 1, 2))):
            source = ref.at[place - CHUNKS[n][0]]
            target = factor.at[slot, :, pl.ds(pl.multiple_of(lax.rem(x_at + turn, 4) * 64, 64), 64), :]
            copies.append(pltpu.make_async_copy(source, target, factor_sems.at[slot, quarter]))
        return copies

    def stores(place):
        slot = place - places[0]
        copies = [pltpu.make_async_copy(solved_buf.at[slot], out_ref.at[table_ref[place]], out_sems.at[slot, 0])]
        if solved_ref is not None:
            at = pl.multiple_of((place - begin) * columns, columns)
            copies.append(
                pltpu.make_async_copy(solved_buf.at[slot], solved_ref.at[pl.ds(at, columns)], out_sems.at[slot, 1])
            )
        return copies

    incoming = [
        pltpu.make_async_copy(
            ref.at[pl.ds(0, CAP * columns)], window.at[pl.ds(n * CAP * columns, CAP * columns)], window_sems.at[n]
        )
        for n, ref in enumerate(windows)
    ]
    for copy in incoming:
        copy.start()
    for place in places:

        @pl.when((place >= begin) & (place < end))
        def _(place=place):
            for copy in fetches(place):
                copy.start()

    for copy in incoming:
        copy.wait()
    for place in places:

        @pl.when((place >= begin) & (place < end))
        def _(place=place):
            slot = place - places[0]
            for copy in fetches(place):
                copy.wait()
            total = jnp.zeros(right_buf.shape[1:], jnp.float32)
            for k in range(8):
                at = pl.multiple_of(table_ref[16 + 8 * place + k] * columns, columns)
                total = total + dot_t(window[pl.ds(at, columns)], factor[slot, k])
            totals[slot] = total

    for place in places:
        slot = place - places[0]
        residue = (right_buf[slot].astype(jnp.float32) - totals[slot]).astype(jnp.bfloat16)
        solved_buf[slot] = dot_t(residue, diag_buf[slot]).astype(solved_buf.dtype)
    for place in places:

        @pl.when((place >= begin) & (place < end))
        def _(place=place):
            for copy in stores(place):
                copy.start()

    for place in places:

        @pl.when((place >= begin) & (place < end))
        def _(place=place):
            for copy in stores(place):
                copy.wait()


def level_call(level, table, right, diag, parts, windows, out):
    rows, columns, size = right.shape
    places = PLACES[level]
    used = sorted({chunk_of(place) for place in places})
    flat = [piece for n in used for piece in parts[n]]
    operands = [table, right, diag, *flat, *windows, out]
    count = len(places)
    return pl.pallas_call(
        functools.partial(level_kernel, level, used),
        out_shape=[
            jax.ShapeDtypeStruct(out.shape, out.dtype),
            jax.ShapeDtypeStruct((CAP * columns, size), out.dtype),
        ][: 1 if level == LEVELS - 1 else 2],
        in_specs=[SMEM] + [ANY] * (len(operands) - 1),
        out_specs=[ANY, ANY][: 1 if level == LEVELS - 1 else 2],
        input_output_aliases={len(operands) - 1: 0},
        scratch_shapes=[
            pltpu.VMEM((4 * level * CAP * columns, size), out.dtype),
            pltpu.VMEM((count, 8, size, size), out.dtype),
            pltpu.VMEM((count, size, size), out.dtype),
            pltpu.VMEM((count, columns, size), out.dtype),
            pltpu.VMEM((count, columns, size), out.dtype),
            pltpu.VMEM((count, columns, size), jnp.float32),
            pltpu.SemaphoreType.DMA((4 * level,)),
            pltpu.SemaphoreType.DMA((count, 4)),
            pltpu.SemaphoreType.DMA((count, 2)),
            pltpu.SemaphoreType.DMA((count, 2)),
        ],
        compiler_params=PARAMS,
        cost_estimate=pl.CostEstimate(
            flops=2 * CAP * 9 * columns * size * size, bytes_accessed=8 * 2**20, transcendentals=0
        ),
    )(*operands)


def round_x(block, distance):
    size = lax.axis_size("rhs")
    return lax.ppermute(block, "rhs", [(i, (i + distance) % size) for i in range(size)])


def up(block, distance):
    size = lax.axis_size("rows")
    return lax.ppermute(block, "rows", [(i, i + distance) for i in range(size - distance)])


def after(value, *others):
    return lax.optimization_barrier((value, others))[0]


def ring(chunk, forward, *before):
    low, high = round_x(chunk, 1), round_x(chunk, -1)
    if forward == 0:
        return [chunk, low, high, round_x(chunk, 2)]
    return [chunk, low, high, round_x(after(low if forward > 0 else high, *before), forward)]


def shift(solved):
    size = lax.axis_size("rows")
    two = up(solved, 2)
    mixed = lax.ppermute(
        solved, "rows", [(i, i + (3 if i % 2 else 1)) for i in range(size) if i + (3 if i % 2 else 1) < size]
    )
    swapped = lax.ppermute(after(two, mixed), "rows", [(i, i ^ 1) for i in range(size)])
    return [solved, swapped, two, mixed]


def per_device(right, off, diag, level, columns):
    x_at = lax.axis_index("rhs").astype(jnp.int32).reshape(1)
    rows_at = lax.axis_index("rows").astype(jnp.int32).reshape(1)
    half = diag.shape[0] // 2
    before, beyond = round_x(diag, 1), round_x(diag, -1)
    chunks = sort_call(level, off)
    low, high = after((before[:half], beyond[half:]), *chunks)
    diag_pieces = [diag, before, beyond, round_x(low, 1), round_x(high, -1)]
    out, diag, solved = first_call(x_at, level, right, diag_pieces)
    windows = shift(solved)
    parts = []
    for chunk, ahead in ((chunks[0], []), (chunks[1], [*diag_pieces])):
        chunk = after(chunk, *ahead)
        parts.append([chunk, round_x(chunk, 1), round_x(chunk, -1)])
    ahead = [solved, *parts[0], *parts[1]]
    parts[0].append(round_x(after(parts[0][1], solved), 1))
    parts[1].append(round_x(after(parts[1][2], *ahead), -1))
    table = table_call(rows_at, x_at, level, columns, windows[1:])
    parts.append(ring(after(chunks[2], *parts[1], *parts[0], table), FORWARD[2]))
    out, solved = level_call(1, table, right, diag, parts, windows, out)
    windows += shift(solved)
    parts.append(ring(after(chunks[3], *parts[2][:3]), FORWARD[3]))
    out, solved = level_call(2, table, right, diag, parts, windows, out)
    windows += shift(solved)
    return level_call(3, table, right, diag, parts, windows, out)[0]


def solution(mesh):
    return jax.shard_map(
        per_device,
        mesh=mesh,
        in_specs=(
            P("rows", "rhs", None),
            P("rows", None, "rhs", None),
            P("rows", "rhs", None),
            P("rows"),
            P("rows", None),
        ),
        out_specs=P("rows", "rhs", None),
        check_vma=False,
    )
```

```python
import functools

import jax
import jax.numpy as jnp
from jax import lax
from jax.experimental import pallas as pl
from jax.experimental.pallas import tpu as pltpu
from jax.sharding import PartitionSpec as P

LEVELS = 4
REACH = 4
CAP = 4
ANY = pl.BlockSpec(memory_space=pl.ANY)
SMEM = pl.BlockSpec(memory_space=pltpu.SMEM)
VMEM = pl.BlockSpec(memory_space=pltpu.VMEM)
PARAMS = pltpu.CompilerParams(vmem_limit_bytes=61 * 2**20)

PLACES = {1: range(0, 4), 2: range(1, 6), 3: range(2, 7), 0: range(4, 8)}
CHUNKS = ((0, 2), (2, 4), (4, 6), (6, 7))
FORWARD = (1, -1, 1, -1)


def order_of(level_ref, order_ref):
    at = jnp.int32(0)
    starts = {}
    for level in (1, 2, 3, 0):
        starts[level] = at
        for row in range(8):
            here = level_ref[row] == level

            @pl.when(here)
            def _(at=at, row=row):
                order_ref[at] = jnp.int32(row)

            at = at + here.astype(jnp.int32)
    return starts


def sort_kernel(level_ref, off_ref, *refs):
    chunks, (order_ref, sems) = refs[: len(CHUNKS)], refs[len(CHUNKS) :]
    order_of(level_ref, order_ref)
    copies = []
    for chunk_ref, (low, high) in zip(chunks, CHUNKS):
        for place in range(low, high):
            copies.append(
                pltpu.make_async_copy(off_ref.at[order_ref[place]], chunk_ref.at[place - low], sems.at[place])
            )
    for copy in copies:
        copy.start()
    for copy in copies:
        copy.wait()


def sort_call(level, off):
    return pl.pallas_call(
        sort_kernel,
        out_shape=[jax.ShapeDtypeStruct((high - low,) + off.shape[1:], off.dtype) for low, high in CHUNKS],
        in_specs=[SMEM, ANY],
        out_specs=[VMEM] * len(CHUNKS),
        scratch_shapes=[pltpu.SMEM((8,), jnp.int32), pltpu.SemaphoreType.DMA((8,))],
        compiler_params=pltpu.CompilerParams(vmem_limit_bytes=60 * 2**20),
    )(level, off)


TABLE = 80
TAIL = 16


def table_kernel(rows_at_ref, x_ref, level_ref, columns_ref, one_ref, two_ref, three_ref, table_ref, slot_ref, levels_ref, near_ref, sem):
    parts = [
        ref[ref.shape[0] - TAIL :, :128].astype(jnp.float32).astype(jnp.int32)[:8] for ref in (one_ref, two_ref, three_ref)
    ]
    lane = lax.broadcasted_iota(jnp.int32, (8, 128), 0)
    levels_ref[...] = jnp.where(lane == 0, parts[0], jnp.where(lane == 1, parts[1], parts[2]))
    copy = pltpu.make_async_copy(levels_ref, near_ref, sem)
    copy.start()
    starts = order_of(level_ref, table_ref)
    ends = {1: starts[2], 2: starts[3], 3: starts[0], 0: jnp.int32(8)}
    for level in range(LEVELS):
        table_ref[8 + level] = starts[level]
        table_ref[12 + level] = ends[level]
    copy.wait()
    for buffer in range(REACH):
        seen = [jnp.int32(0)] * LEVELS
        for row in range(8):
            level = level_ref[row] if buffer == 0 else near_ref[buffer - 1, row] & 3
            rank = jnp.int32(0)
            for other in range(LEVELS):
                here = level == other
                rank = jnp.where(here, seen[other], rank)
                seen[other] = seen[other] + here.astype(jnp.int32)
            slot_ref[buffer * 8 + row] = 16 * jnp.minimum(level, 2) + 4 * buffer + jnp.minimum(rank, CAP - 1)
    base = rows_at_ref[0]
    table_ref[72] = x_ref[0]
    for place in range(7):
        row = table_ref[place]
        for k in range(8):
            column = columns_ref[row, k]
            distance = jnp.clip(base - lax.shift_right_logical(column, 3), 0, REACH - 1)
            buffer = jnp.where((base & distance & 1) == 1, 4 - distance, distance)
            table_ref[16 + 8 * place + k] = slot_ref[buffer * 8 + (column & 7)]


def table_call(rows_at, x_at, level, columns, received):
    return pl.pallas_call(
        table_kernel,
        out_shape=jax.ShapeDtypeStruct((TABLE,), jnp.int32),
        in_specs=[SMEM] * 4 + [VMEM] * 3,
        out_specs=SMEM,
        scratch_shapes=[
            pltpu.SMEM((32,), jnp.int32),
            pltpu.VMEM((8, 128), jnp.int32),
            pltpu.SMEM((8, 128), jnp.int32),
            pltpu.SemaphoreType.DMA,
        ],
        compiler_params=PARAMS,
        cost_estimate=pl.CostEstimate(flops=10**9, bytes_accessed=2**20, transcendentals=0),
    )(rows_at, x_at, level, columns, *received)


def dot_t(x, y):
    return lax.dot_general(x, y, (((1,), (1,)), ((), ())), preferred_element_type=jnp.float32)


def first_kernel(
    x_ref, level_ref, right_ref, own_ref, before_ref, after_ref, low_ref, high_ref,
    out_ref, diag_ref, solved_ref,
    order_ref, inverse, right_buf, solved_buf, tail_buf, sems, right_sems, out_sems, diag_sem, tail_sem,
):
    x_at = x_ref[0]
    columns = right_ref.shape[1]
    half = low_ref.shape[0]
    whole, low, high = pl.ds(0, 2 * half), pl.ds(0, half), pl.ds(half, half)
    sources = ((own_ref, 0, whole), (before_ref, 3, whole), (after_ref, 1, whole), (low_ref, 2, low), (high_ref, 2, high))
    pieces = []
    for n, (ref, turn, rows) in enumerate(sources):
        at = pl.multiple_of(lax.rem(x_at + turn, 4) * 64, 64)
        pieces.append(pltpu.make_async_copy(ref, inverse.at[rows, pl.ds(at, 64)], sems.at[n]))
    for piece in pieces:
        piece.start()
    begin = order_of(level_ref, order_ref)[0]

    def fetch(place):
        return pltpu.make_async_copy(
            right_ref.at[order_ref[place]], right_buf.at[place - 4], right_sems.at[place - 4]
        )

    def stores(place):
        at = pl.multiple_of((place - begin) * columns, columns)
        source = solved_buf.at[place - 4]
        return [
            pltpu.make_async_copy(source, solved_ref.at[pl.ds(at, columns)], out_sems.at[place - 4, 0]),
            pltpu.make_async_copy(source, out_ref.at[order_ref[place]], out_sems.at[place - 4, 1]),
        ]

    for place in PLACES[0]:

        @pl.when(place >= begin)
        def _(place=place):
            fetch(place).start()

    lane = lax.broadcasted_iota(jnp.int32, (TAIL, 256), 1)
    tail = jnp.zeros((TAIL, 256), jnp.int32)
    for row in range(8):
        tail = jnp.where(lane == row, level_ref[row], tail)
    tail_buf[...] = tail.astype(jnp.float32).astype(tail_buf.dtype)
    levels = pltpu.make_async_copy(tail_buf, solved_ref.at[pl.ds(CAP * columns, TAIL)], tail_sem)
    levels.start()
    for piece in pieces:
        piece.wait()
    whole = pltpu.make_async_copy(inverse, diag_ref, diag_sem)
    whole.start()
    for place in PLACES[0]:

        @pl.when(place >= begin)
        def _(place=place):
            fetch(place).wait()
            solved_buf[place - 4] = dot_t(right_buf[place - 4], inverse[order_ref[place]]).astype(solved_buf.dtype)
            for copy in stores(place):
                copy.start()

    for place in PLACES[0]:

        @pl.when(place >= begin)
        def _(place=place):
            for copy in stores(place):
                copy.wait()

    levels.wait()
    whole.wait()


def first_call(x_at, level, right, diag_pieces):
    rows, columns, size = right.shape
    return pl.pallas_call(
        first_kernel,
        out_shape=[
            jax.ShapeDtypeStruct(right.shape, right.dtype),
            jax.ShapeDtypeStruct((rows, size, size), right.dtype),
            jax.ShapeDtypeStruct((CAP * columns + TAIL, size), right.dtype),
        ],
        in_specs=[SMEM, SMEM] + [ANY] * 6,
        out_specs=[ANY, ANY, ANY],
        scratch_shapes=[
            pltpu.SMEM((8,), jnp.int32),
            pltpu.VMEM((rows, size, size), right.dtype),
            pltpu.VMEM((CAP, columns, size), right.dtype),
            pltpu.VMEM((CAP, columns, size), right.dtype),
            pltpu.VMEM((TAIL, size), right.dtype),
            pltpu.SemaphoreType.DMA((5,)),
            pltpu.SemaphoreType.DMA((CAP,)),
            pltpu.SemaphoreType.DMA((CAP, 2)),
            pltpu.SemaphoreType.DMA,
            pltpu.SemaphoreType.DMA,
        ],
        compiler_params=PARAMS,
        cost_estimate=pl.CostEstimate(flops=2 * CAP * columns * size * size, bytes_accessed=3 * 2**20, transcendentals=0),
    )(x_at, level, right, *diag_pieces)


def chunk_of(place):
    return next(n for n, (low, high) in enumerate(CHUNKS) if low <= place < high)


def level_kernel(level, used, table_ref, right_ref, diag_ref, *refs):
    places = PLACES[level]
    refs = list(refs)

    def take(count):
        taken = refs[:count]
        del refs[:count]
        return taken

    parts = {n: take(4) for n in used}
    windows = take(4 * level)
    take(1)
    out_ref = take(1)[0]
    solved_ref = take(1)[0] if level < LEVELS - 1 else None
    window, factor, diag_buf, right_buf, solved_buf, totals, window_sems, factor_sems, row_sems, out_sems = refs
    columns = right_ref.shape[1]
    x_at = table_ref[72]
    begin, end = table_ref[8 + level], table_ref[12 + level]

    def fetches(place):
        slot = place - places[0]
        row = table_ref[place]
        copies = [
            pltpu.make_async_copy(right_ref.at[row], right_buf.at[slot], row_sems.at[slot, 0]),
            pltpu.make_async_copy(diag_ref.at[row], diag_buf.at[slot], row_sems.at[slot, 1]),
        ]
        n = chunk_of(place)
        for quarter, (ref, turn) in enumerate(zip(parts[n], (0, 3, 1, 2))):
            source = ref.at[place - CHUNKS[n][0]]
            target = factor.at[slot, :, pl.ds(pl.multiple_of(lax.rem(x_at + turn, 4) * 64, 64), 64), :]
            copies.append(pltpu.make_async_copy(source, target, factor_sems.at[slot, quarter]))
        return copies

    def stores(place):
        slot = place - places[0]
        copies = [pltpu.make_async_copy(solved_buf.at[slot], out_ref.at[table_ref[place]], out_sems.at[slot, 0])]
        if solved_ref is not None:
            at = pl.multiple_of((place - begin) * columns, columns)
            copies.append(
                pltpu.make_async_copy(solved_buf.at[slot], solved_ref.at[pl.ds(at, columns)], out_sems.at[slot, 1])
            )
        return copies

    incoming = [
        pltpu.make_async_copy(
            ref.at[pl.ds(0, CAP * columns)], window.at[pl.ds(n * CAP * columns, CAP * columns)], window_sems.at[n]
        )
        for n, ref in enumerate(windows)
    ]
    for copy in incoming:
        copy.start()
    for place in places:

        @pl.when((place >= begin) & (place < end))
        def _(place=place):
            for copy in fetches(place):
                copy.start()

    for copy in incoming:
        copy.wait()
    for place in places:

        @pl.when((place >= begin) & (place < end))
        def _(place=place):
            slot = place - places[0]
            for copy in fetches(place):
                copy.wait()
            total = jnp.zeros(right_buf.shape[1:], jnp.float32)
            for k in range(8):
                at = pl.multiple_of(table_ref[16 + 8 * place + k] * columns, columns)
                total = total + dot_t(window[pl.ds(at, columns)], factor[slot, k])
            totals[slot] = total

    for place in places:
        slot = place - places[0]
        residue = (right_buf[slot].astype(jnp.float32) - totals[slot]).astype(jnp.bfloat16)
        solved_buf[slot] = dot_t(residue, diag_buf[slot]).astype(solved_buf.dtype)
    for place in places:

        @pl.when((place >= begin) & (place < end))
        def _(place=place):
            for copy in stores(place):
                copy.start()

    for place in places:

        @pl.when((place >= begin) & (place < end))
        def _(place=place):
            for copy in stores(place):
                copy.wait()


def level_call(level, table, right, diag, parts, windows, out):
    rows, columns, size = right.shape
    places = PLACES[level]
    used = sorted({chunk_of(place) for place in places})
    flat = [piece for n in used for piece in parts[n]]
    operands = [table, right, diag, *flat, *windows, out]
    count = len(places)
    return pl.pallas_call(
        functools.partial(level_kernel, level, used),
        out_shape=[
            jax.ShapeDtypeStruct(out.shape, out.dtype),
            jax.ShapeDtypeStruct((CAP * columns, size), out.dtype),
        ][: 1 if level == LEVELS - 1 else 2],
        in_specs=[SMEM] + [ANY] * (len(operands) - 1),
        out_specs=[ANY, ANY][: 1 if level == LEVELS - 1 else 2],
        input_output_aliases={len(operands) - 1: 0},
        scratch_shapes=[
            pltpu.VMEM((4 * level * CAP * columns, size), out.dtype),
            pltpu.VMEM((count, 8, size, size), out.dtype),
            pltpu.VMEM((count, size, size), out.dtype),
            pltpu.VMEM((count, columns, size), out.dtype),
            pltpu.VMEM((count, columns, size), out.dtype),
            pltpu.VMEM((count, columns, size), jnp.float32),
            pltpu.SemaphoreType.DMA((4 * level,)),
            pltpu.SemaphoreType.DMA((count, 4)),
            pltpu.SemaphoreType.DMA((count, 2)),
            pltpu.SemaphoreType.DMA((count, 2)),
        ],
        compiler_params=PARAMS,
        cost_estimate=pl.CostEstimate(
            flops=2 * CAP * 9 * columns * size * size, bytes_accessed=8 * 2**20, transcendentals=0
        ),
    )(*operands)


def round_x(block, distance):
    size = lax.axis_size("rhs")
    return lax.ppermute(block, "rhs", [(i, (i + distance) % size) for i in range(size)])


def up(block, distance):
    size = lax.axis_size("rows")
    return lax.ppermute(block, "rows", [(i, i + distance) for i in range(size - distance)])


def after(value, *others):
    return lax.optimization_barrier((value, others))[0]


def ring(chunk, forward, *before):
    low, high = round_x(chunk, 1), round_x(chunk, -1)
    if forward == 0:
        return [chunk, low, high, round_x(chunk, 2)]
    return [chunk, low, high, round_x(after(low if forward > 0 else high, *before), forward)]


def shift(solved):
    size = lax.axis_size("rows")
    two = up(solved, 2)
    mixed = lax.ppermute(
        solved, "rows", [(i, i + (3 if i % 2 else 1)) for i in range(size) if i + (3 if i % 2 else 1) < size]
    )
    swapped = lax.ppermute(after(two, mixed), "rows", [(i, i ^ 1) for i in range(size)])
    return [solved, swapped, two, mixed]


def per_device(right, off, diag, level, columns):
    x_at = lax.axis_index("rhs").astype(jnp.int32).reshape(1)
    rows_at = lax.axis_index("rows").astype(jnp.int32).reshape(1)
    half = diag.shape[0] // 2
    before, beyond = round_x(diag, 1), round_x(diag, -1)
    chunks = sort_call(level, off)
    low, high = after((before[:half], beyond[half:]), *chunks)
    diag_pieces = [diag, before, beyond, round_x(low, 1), round_x(high, -1)]
    out, diag, solved = first_call(x_at, level, right, diag_pieces)
    windows = shift(solved)
    parts = []
    for chunk, ahead in ((chunks[0], []), (chunks[1], [*diag_pieces])):
        chunk = after(chunk, *ahead)
        parts.append([chunk, round_x(chunk, 1), round_x(chunk, -1)])
    ahead = [solved, *parts[0], *parts[1]]
    parts[0].append(round_x(after(parts[0][1], solved), 1))
    parts[1].append(round_x(after(parts[1][2], *ahead), -1))
    table = table_call(rows_at, x_at, level, columns, windows[1:])
    parts.append(ring(after(chunks[2], *parts[1], *parts[0], table), FORWARD[2]))
    out, solved = level_call(1, table, right, diag, parts, windows, out)
    windows += shift(solved)
    parts.append(ring(after(chunks[3], *parts[2][:3]), FORWARD[3]))
    out, solved = level_call(2, table, right, diag, parts, windows, out)
    windows += shift(solved)
    return level_call(3, table, right, diag, parts, windows, out)[0]


def solution(mesh):
    return jax.shard_map(
        per_device,
        mesh=mesh,
        in_specs=(
            P("rows", "rhs", None),
            P("rows", None, "rhs", None),
            P("rows", "rhs", None),
            P("rows"),
            P("rows", None),
        ),
        out_specs=P("rows", "rhs", None),
        check_vma=False,
    )
```
